32 devices in a mesh: disc: 2 (over x), phi: 16 (over z, y, core).
Axes of the slice: x: 2, y: 2, z: 4, core: 2. Of those that a mesh axis runs over, the one named last changes fastest.
Arguments:
- density: float32 [16, 3072, 1024], P('disc', 'phi'), parts along dimension 0, may hold values from 0.05 to 2
- frag_rate: float32 [16, 3072], P('disc', 'phi'), parts along dimension 0, may hold values from 0.05 to 0.5
- radial_speed: float32 [1024], replicated, may hold values from 0.05 to 0.4
- azimuth_speed: float32 [1024], replicated, may hold values from -0.45 to 0.45
- fraction: float32 [16], P('disc'), parts along dimension 0, may hold values from 0 to 1
- shifts: int32 [16], P('disc'), parts along dimension 0, may hold values from 0 to 3071, as said below
- pivots: int32 [1024], replicated, may hold values from 0 to 1022, as said below
Outputs:
- remapped: float32 [16, 3072, 1024], P('disc', 'phi'), parts along dimension 0
The draws below stay inside these ranges and needn't reach their ends.
There are 2 independent parts, one for each index of `disc`. The reference program is written for one: setup_inputs(seed, part) draws one part's arguments, and reference() takes and returns one part's arrays. A program takes and returns all parts, laid end to end along the dimension named above; an argument that names none is the same for every part. Nothing has to cross between parts.
Inputs may be any that keep to these rules, and one draw needn't show every extreme that they name: `shifts`: each radius moves its dust by this many whole cells toward higher azimuth indices. pivots[0] is 0 and pivots[j] < j for every other bin j.
All inputs are finite; a program needn't handle non-finite values.
Results may differ from the reference program's by a relative error of at most 0.000064.
Values sent between devices are 32-bit elements; how exact they have to be, the bound alone decides.
A program may use at most 128 MiB of HBM per device.

```python
import math
import jax
import jax.numpy as jnp
from jax import lax

NR = 8
A_DEV = 192
NB = 1024
NA = 3072
N_PHI = 16


def draw_shifts(key, part):
    cycle_size = N_PHI
    bit_count = max((cycle_size - 1).bit_length(), 1)
    key_hops, key_rest = jax.random.split(jax.random.fold_in(key, 7))
    device_hops = jax.random.randint(key_hops, (NR,), 0, cycle_size)
    forced = jnp.left_shift(jnp.int32(1), jnp.arange(NR, dtype=jnp.int32) % bit_count)
    device_hops = jnp.bitwise_or(device_hops, forced) % cycle_size
    cell_rest = jax.random.randint(key_rest, (NR,), 0, A_DEV)
    result = device_hops * A_DEV + cell_rest
    result = jnp.where(jnp.arange(NR) == NR - 1, NA - 1, result)
    return result.astype(jnp.int32)


def draw_pivots(key, part):
    bins = jnp.arange(NB, dtype=jnp.int32)
    result = jax.random.randint(jax.random.fold_in(key, 3), (NB,), 0, jnp.maximum(bins, 1))
    result = jnp.where(bins == NB - 1, NB - 2, result)
    return result.astype(jnp.int32)


def shard_levels(key, shape, shards, least, largest):
    level = 1.0
    for position, blocks in shards:
        steps = jax.random.uniform(jax.random.fold_in(jax.random.fold_in(key, 6), position), (blocks,), jnp.float32, least / len(shards), largest / len(shards))
        level = level * jnp.repeat(jnp.exp(steps), shape[position] // blocks).reshape((-1,) + (1,) * (len(shape) - 1 - position))
    return level


def setup_inputs(seed: int = 0, part: int = 0) -> dict:
    streams_of = jax.random.split(jax.random.key(seed), 8)
    part_keys = jax.random.split(jax.random.fold_in(streams_of[7], part), 8)
    density = jnp.clip(jnp.exp(math.log(2.0) - 3.6888794 * jax.random.uniform(part_keys[0], (NR, NA, NB), jnp.float32) ** shard_levels(part_keys[0], (NR, NA, NB), ((1, 16),), -0.2, 0.2)), 0.05, 2.0)
    frag_rate = jnp.clip(jnp.exp(math.log(0.5) - 2.3025851 * jax.random.uniform(part_keys[1], (NR, NA), jnp.float32) ** shard_levels(part_keys[1], (NR, NA), ((1, 16),), -0.2, 0.2)), 0.05, 0.5)
    radial_speed = jnp.clip(jnp.exp(jax.random.uniform(streams_of[2], (NB,), jnp.float32, math.log(0.05), math.log(0.4))), 0.05, 0.4)
    azimuth_speed = jnp.clip(jax.random.uniform(streams_of[3], (NB,), jnp.float32, -0.45, 0.45), -0.45, 0.45)
    fraction = jnp.clip(jax.random.uniform(part_keys[4], (NR,), jnp.float32, 0.0, 1.0), 0.0, 1.0)
    shifts = draw_shifts(jax.random.fold_in(jax.random.fold_in(streams_of[7], part), 71), part)
    pivots = draw_pivots(jax.random.fold_in(streams_of[7], 71), part)
    return {"density": density, "frag_rate": frag_rate, "radial_speed": radial_speed, "azimuth_speed": azimuth_speed, "fraction": fraction, "shifts": shifts, "pivots": pivots}


def breakup_table(pivots, bins):
    source = lax.broadcasted_iota(jnp.int32, (bins, bins), 0)
    target = lax.broadcasted_iota(jnp.int32, (bins, bins), 1)
    share = 1.0 / (pivots.astype(jnp.float32) + 1.0)
    active = source >= 1
    gain = jnp.where((target <= pivots[:, None]) & active, share[:, None], jnp.float32(0.0))
    loss = jnp.where((target == source) & active, jnp.float32(1.0), jnp.float32(0.0))
    return (gain - loss).astype(jnp.float32)


def roll_cells(field, offset):
    return jnp.roll(field, offset, axis=0)


def reference(density, frag_rate, radial_speed, azimuth_speed, fraction, shifts, pivots):
    inward = jnp.concatenate([density[1:], jnp.zeros_like(density[:1])], axis=0)
    settled = (1.0 - radial_speed) * density + radial_speed * inward
    forward = jnp.maximum(azimuth_speed, 0.0)
    backward = jnp.maximum(-azimuth_speed, 0.0)
    drifted = (1.0 - jnp.abs(azimuth_speed)) * settled + forward * jnp.roll(settled, 1, axis=1) + backward * jnp.roll(settled, -1, axis=1)
    breakup = breakup_table(pivots, NB)
    flat = drifted.reshape(-1, NB)
    gained = jnp.dot(flat, breakup, precision=lax.Precision.HIGHEST, preferred_element_type=jnp.float32).reshape(drifted.shape)
    broken = drifted + frag_rate[:, :, None] * gained
    first = jax.vmap(roll_cells)(broken, shifts)
    second = jax.vmap(roll_cells)(broken, shifts + 1)
    far_weight = fraction[:, None, None]
    return (1.0 - far_weight) * first + far_weight * second
```

```python
import functools
import jax
import jax.numpy as jnp
from jax import lax
from jax.experimental import pallas as pl
from jax.experimental.pallas import tpu as pltpu
from jax.sharding import PartitionSpec as P


def passed(shard, axis, by):
    count = lax.axis_size(axis)
    return lax.ppermute(shard, axis, [(i, (i + by) % count) for i in range(count)])


def disc_kernel(
    front, cells, start_ref, far_ref, before, own, after, before_in, own_in, after_in,
    frag, radial, azimuth, pivots, out, mask, settled, window, broken,
):
    step = pl.program_id(0)
    back = after.shape[1]
    span = window.shape[0]
    rows = broken.shape[0]
    bins = own.shape[2]

    @pl.when(step == 0)
    def _():
        chunk = 128

        @pl.loop(0, bins // chunk)
        def _(part):
            at = pl.ds(pl.multiple_of(part * chunk, chunk), chunk)
            source = lax.broadcasted_iota(jnp.int32, (chunk, bins), 0) + part * chunk
            target = lax.broadcasted_iota(jnp.int32, (chunk, bins), 1)
            hit = (target <= pivots[at, :]) & (source >= 1)
            mask[at, :] = jnp.where(hit, 1.0, 0.0).astype(jnp.bfloat16)

    speed = radial[0:1, :]
    stay = 1.0 - speed
    gain = jnp.where(step == pl.num_programs(0) - 1, 0.0, speed)
    settled[0:front, :] = stay * before[0] + gain * before_in[0]
    settled[front:front + cells, :] = stay * own[0] + gain * own_in[0]
    settled[front + cells:front + cells + back, :] = stay * after[0] + gain * after_in[0]
    settled[front + cells + back:, :] = jnp.zeros((settled.shape[0] - front - cells - back, bins), jnp.float32)

    start = start_ref[step]
    base = pl.multiple_of((start // 8) * 8, 8)
    window[...] = pltpu.roll(settled[pl.ds(base, span), :], span - lax.rem(start, 8), 0)
    drift = azimuth[0:1, :]
    drifted = (
        (1.0 - jnp.abs(drift)) * window[1:1 + rows, :]
        + jnp.maximum(drift, 0.0) * window[0:rows, :]
        + jnp.maximum(-drift, 0.0) * window[2:2 + rows, :]
    )
    share = azimuth[1:2, :]
    scaled = drifted * share
    high = scaled.astype(jnp.bfloat16)
    low = (scaled - high.astype(jnp.float32)).astype(jnp.bfloat16)
    gained = jnp.dot(high, mask[...], preferred_element_type=jnp.float32)
    gained += jnp.dot(low, mask[...], preferred_element_type=jnp.float32)
    column = lax.broadcasted_iota(jnp.int32, (1, bins), 1)
    lost = jnp.where(column >= 1, 1.0, 0.0)
    broken[...] = drifted + frag[0] * (gained - lost * drifted)
    far = far_ref[step]
    out[0] = (1.0 - far) * broken[1:1 + cells, :] + far * broken[0:cells, :]


def aligned_blocks(density, frag_rate, radial_speed, azimuth_speed, fraction, rest, pivots):
    radii, cells, bins = density.shape
    half = cells // 2
    front = -(-(half + 2) // 8) * 8
    back = half
    before = passed(density[:, cells - front:], "phi", 1)
    after = passed(density[:, :back], "phi", -1)
    frag_before = passed(frag_rate[:, cells - front:], "phi", 1)
    frag_after = passed(frag_rate[:, :back], "phi", -1)
    start = front - 2 - rest
    rows = cells + 8
    span = cells + 16
    pad = jnp.zeros((radii, 16), jnp.float32)
    frag_all = jnp.concatenate([frag_before, frag_rate, frag_after, pad], axis=1)
    frag = jax.vmap(lambda row, at: lax.dynamic_slice_in_dim(row, at, rows))(frag_all, start + 1)[:, :, None]
    share = 1.0 / (pivots.astype(jnp.float32) + 1.0)
    speeds = jnp.stack([azimuth_speed, share])
    last = radii - 1
    here = lambda r: (r, 0, 0)
    inner = lambda r: (jnp.minimum(r + 1, last), 0, 0)
    fixed = lambda r: (0, 0)
    smem = pl.BlockSpec(memory_space=pltpu.SMEM)
    return pl.pallas_call(
        functools.partial(disc_kernel, front, cells),
        grid=(radii,),
        in_specs=[
            smem, smem,
            pl.BlockSpec((1, front, bins), here),
            pl.BlockSpec((1, cells, bins), here),
            pl.BlockSpec((1, back, bins), here),
            pl.BlockSpec((1, front, bins), inner),
            pl.BlockSpec((1, cells, bins), inner),
            pl.BlockSpec((1, back, bins), inner),
            pl.BlockSpec((1, rows, 1), here),
            pl.BlockSpec((1, bins), fixed),
            pl.BlockSpec((2, bins), fixed),
            pl.BlockSpec((bins, 1), fixed),
        ],
        out_specs=pl.BlockSpec((1, cells, bins), here),
        out_shape=jax.ShapeDtypeStruct((radii, cells, bins), jnp.float32),
        scratch_shapes=[
            pltpu.VMEM((bins, bins), jnp.bfloat16),
            pltpu.VMEM((front + cells + back + 16, bins), jnp.float32),
            pltpu.VMEM((span, bins), jnp.float32),
            pltpu.VMEM((rows, bins), jnp.float32),
        ],
        compiler_params=pltpu.CompilerParams(vmem_limit_bytes=40 * 2**20),
        cost_estimate=pl.CostEstimate(
            flops=4 * radii * rows * bins * bins, bytes_accessed=6 * 4 * radii * cells * bins, transcendentals=0
        ),
    )(
        start, fraction, before, density, after, before, density, after,
        frag, radial_speed[None], speeds, pivots[:, None],
    )


def carry(blocks, hops):
    count = lax.axis_size("phi")
    moves = [functools.partial(passed, axis="phi", by=by) if by else (lambda block: block) for by in range(count)]

    def one(r, result):
        block = lax.dynamic_slice_in_dim(blocks, r, 1, 0)
        landed = lax.switch(hops[r], moves, block)
        return lax.dynamic_update_slice_in_dim(result, landed, r, 0)

    return lax.fori_loop(0, blocks.shape[0], one, jnp.zeros_like(blocks))


def body(density, frag_rate, radial_speed, azimuth_speed, fraction, shifts, pivots):
    cells = density.shape[1]
    count = lax.axis_size("phi")
    rest = shifts % cells
    ahead = (rest > cells // 2).astype(jnp.int32)
    hops = (shifts // cells + ahead) % count
    rest = rest - cells * ahead
    blocks = aligned_blocks(density, frag_rate, radial_speed, azimuth_speed, fraction, rest, pivots)
    return carry(blocks, hops)


def solution(mesh):
    placed = (P("disc", "phi", None), P("disc", "phi"), P(), P(), P("disc"), P("disc"), P())
    return jax.shard_map(
        body, mesh=mesh, in_specs=placed, out_specs=P("disc", "phi", None), check_vma=False
    )
```

```python
import functools
import jax
import jax.numpy as jnp
from jax import lax
from jax.experimental import pallas as pl
from jax.experimental.pallas import tpu as pltpu
from jax.sharding import PartitionSpec as P


def passed(shard, axis, by):
    count = lax.axis_size(axis)
    if by % count == 0:
        return shard
    return lax.ppermute(shard, axis, [(i, (i + by) % count) for i in range(count)])


def disc_kernel(own, own_in, edges, edges_in, frag, radial, azimuth, pivots, out, mask, window):
    step = pl.program_id(0)
    cells, bins = own.shape[1:]

    @pl.when(step == 0)
    def _():
        chunk = 128

        @pl.loop(0, bins // chunk)
        def _(part):
            at = pl.ds(pl.multiple_of(part * chunk, chunk), chunk)
            source = lax.broadcasted_iota(jnp.int32, (chunk, bins), 0) + part * chunk
            target = lax.broadcasted_iota(jnp.int32, (chunk, bins), 1)
            hit = (target <= pivots[at, :]) & (source >= 1)
            mask[at, :] = jnp.where(hit, 1.0, 0.0).astype(jnp.bfloat16)

    speed = radial[0:1, :]
    stay = 1.0 - speed
    gain = jnp.where(step == pl.num_programs(0) - 1, 0.0, speed)
    window[7:8, :] = stay * edges[0, 0:1, :] + gain * edges_in[0, 0:1, :]
    window[8:8 + cells, :] = stay * own[0] + gain * own_in[0]
    window[8 + cells:9 + cells, :] = stay * edges[0, 1:2, :] + gain * edges_in[0, 1:2, :]
    drift = azimuth[0:1, :]
    drifted = (
        (1.0 - jnp.abs(drift)) * window[8:8 + cells, :]
        + jnp.maximum(drift, 0.0) * window[7:7 + cells, :]
        + jnp.maximum(-drift, 0.0) * window[9:9 + cells, :]
    )
    share = azimuth[1:2, :]
    scaled = drifted * share
    high = scaled.astype(jnp.bfloat16)
    low = (scaled - high.astype(jnp.float32)).astype(jnp.bfloat16)
    gained = jnp.dot(high, mask[...], preferred_element_type=jnp.float32)
    gained += jnp.dot(low, mask[...], preferred_element_type=jnp.float32)
    column = lax.broadcasted_iota(jnp.int32, (1, bins), 1)
    lost = jnp.where(column >= 1, 1.0, 0.0)
    out[0] = drifted + frag[0] * (gained - lost * drifted)


def broken_blocks(density, frag_rate, radial_speed, azimuth_speed, pivots):
    radii, cells, bins = density.shape
    before = passed(density[:, cells - 1], "phi", 1)
    after = passed(density[:, 0], "phi", -1)
    edges = jnp.stack([before, after], axis=1)
    share = 1.0 / (pivots.astype(jnp.float32) + 1.0)
    speeds = jnp.stack([azimuth_speed, share])
    last = radii - 1
    here = lambda r: (r, 0, 0)
    inner = lambda r: (jnp.minimum(r + 1, last), 0, 0)
    fixed = lambda r: (0, 0)
    return pl.pallas_call(
        disc_kernel,
        grid=(radii,),
        in_specs=[
            pl.BlockSpec((1, cells, bins), here),
            pl.BlockSpec((1, cells, bins), inner),
            pl.BlockSpec((1, 2, bins), here),
            pl.BlockSpec((1, 2, bins), inner),
            pl.BlockSpec((1, cells, 1), here),
            pl.BlockSpec((1, bins), fixed),
            pl.BlockSpec((2, bins), fixed),
            pl.BlockSpec((bins, 1), fixed),
        ],
        out_specs=pl.BlockSpec((1, cells, bins), here),
        out_shape=jax.ShapeDtypeStruct((radii, cells, bins), jnp.float32),
        scratch_shapes=[
            pltpu.VMEM((bins, bins), jnp.bfloat16),
            pltpu.VMEM((cells + 16, bins), jnp.float32),
        ],
        compiler_params=pltpu.CompilerParams(vmem_limit_bytes=40 * 2**20),
        cost_estimate=pl.CostEstimate(
            flops=4 * radii * cells * bins * bins, bytes_accessed=3 * 4 * radii * cells * bins, transcendentals=0
        ),
    )(
        density, density, edges, edges, frag_rate[:, :, None],
        radial_speed[None], speeds, pivots[:, None],
    )


def mix_kernel(place, far_ref, arrived, result, out):
    cells = out.shape[1]
    r = place[0]
    start = place[1]
    base = pl.multiple_of((start // 8) * 8, 8)
    span = cells + 8
    near = pltpu.roll(arrived[pl.ds(base, span), :], lax.rem(span - lax.rem(start, 8), span), 0)
    far = far_ref[r]
    out[0] = (1.0 - far) * near[1:1 + cells] + far * near[0:cells]


def mixed(result, arrived, r, start, fraction):
    radii, cells, bins = result.shape
    return pl.pallas_call(
        mix_kernel,
        grid_spec=pltpu.PrefetchScalarGridSpec(
            num_scalar_prefetch=1,
            grid=(1,),
            in_specs=[
                pl.BlockSpec(memory_space=pltpu.SMEM),
                pl.BlockSpec(arrived.shape, lambda i, place: (0, 0)),
                pl.BlockSpec(memory_space=pl.ANY),
            ],
            out_specs=pl.BlockSpec((1, cells, bins), lambda i, place: (place[0], 0, 0)),
        ),
        out_shape=jax.ShapeDtypeStruct(result.shape, jnp.float32),
        input_output_aliases={3: 0},
        compiler_params=pltpu.CompilerParams(vmem_limit_bytes=16 * 2**20),
        cost_estimate=pl.CostEstimate(
            flops=3 * cells * bins, bytes_accessed=2 * 4 * cells * bins, transcendentals=0
        ),
    )(jnp.stack([r, start]), fraction, arrived, result)


def carry(blocks, fraction, shifts):
    radii, cells, bins = blocks.shape
    count = lax.axis_size("phi")
    parts = next(k for k in (8, 4, 2, 1) if cells % (8 * k) == 0 and (k == 1 or k * count <= 128))
    piece = cells // parts

    def move(place, block):
        hop, part = divmod(place, parts)
        tail = passed(block[cells - (part + 1) * piece:], "phi", hop + 1)
        head = passed(block[:cells - part * piece], "phi", hop)
        return jnp.concatenate([tail, head], axis=0)

    moves = [functools.partial(move, place) for place in range(count * parts)]

    def one(r, result):
        block = lax.dynamic_index_in_dim(blocks, r, 0, keepdims=False)
        shift = shifts[r]
        arrived = lax.switch(shift // piece, moves, block)
        return mixed(result, arrived, r, piece - 1 - shift % piece, fraction)

    return lax.fori_loop(0, radii, one, jnp.zeros_like(blocks))


def body(density, frag_rate, radial_speed, azimuth_speed, fraction, shifts, pivots):
    blocks = broken_blocks(density, frag_rate, radial_speed, azimuth_speed, pivots)
    return carry(blocks, fraction, shifts)


def solution(mesh):
    placed = (P("disc", "phi", None), P("disc", "phi"), P(), P(), P("disc"), P("disc"), P())
    return jax.shard_map(
        body, mesh=mesh, in_specs=placed, out_specs=P("disc", "phi", None), check_vma=False
    )
```

```python
import functools
import jax
import jax.numpy as jnp
from jax import lax
from jax.experimental import pallas as pl
from jax.experimental.pallas import tpu as pltpu
from jax.sharding import PartitionSpec as P


def passed(shard, axis, by):
    count = lax.axis_size(axis)
    if by % count == 0:
        return shard
    return lax.ppermute(shard, axis, [(i, (i + by) % count) for i in range(count)])


def pack_kernel(half, place, own, own_in, radial, out):
    slot = pl.program_id(0)
    radii = pl.num_programs(0)
    cells = own.shape[1]
    r = place[slot]
    first = pl.multiple_of(jnp.where(slot < place[radii], cells - half, 0), 8)
    speed = radial[0:1, :]
    gain = jnp.where(r == radii - 1, 0.0, speed)
    rows = pl.ds(first, half)
    out[0] = (1.0 - speed) * own[0, rows, :] + gain * own_in[0, rows, :]


def packed(density, radial_speed, order, forward_count, half):
    radii, cells, bins = density.shape
    last = radii - 1
    place = jnp.concatenate([order, forward_count[None]])
    return pl.pallas_call(
        functools.partial(pack_kernel, half),
        grid_spec=pltpu.PrefetchScalarGridSpec(
            num_scalar_prefetch=1,
            grid=(radii,),
            in_specs=[
                pl.BlockSpec((1, cells, bins), lambda j, place: (place[j], 0, 0)),
                pl.BlockSpec((1, cells, bins), lambda j, place: (jnp.minimum(place[j] + 1, last), 0, 0)),
                pl.BlockSpec((1, bins), lambda j, place: (0, 0)),
            ],
            out_specs=pl.BlockSpec((1, half, bins), lambda j, place: (j, 0, 0)),
        ),
        out_shape=jax.ShapeDtypeStruct((radii, half, bins), jnp.float32),
        compiler_params=pltpu.CompilerParams(vmem_limit_bytes=16 * 2**20),
        cost_estimate=pl.CostEstimate(
            flops=3 * radii * half * bins, bytes_accessed=10 * radii * cells * bins, transcendentals=0
        ),
    )(place, density, density, radial_speed[None])


def exchanged(slabs, forward_count):
    radii = slabs.shape[0]

    def move(forward, slabs):
        sides = []
        if forward > 0:
            sides.append(passed(slabs[:forward], "phi", 1))
        if forward < radii:
            sides.append(passed(slabs[forward:], "phi", -1))
        return jnp.concatenate(sides, axis=0)

    return lax.switch(forward_count, [functools.partial(move, n) for n in range(radii + 1)], slabs)


def disc_kernel(
    place, far_ref, own, own_in, halo, edges, edges_in, frag, radial, azimuth, pivots,
    out, mask, settled, window, rates, broken,
):
    step = pl.program_id(0)
    radii = pl.num_programs(0)
    cells, bins = own.shape[1:]
    half = halo.shape[1]
    rows = broken.shape[0]
    span = window.shape[0]

    @pl.when(step == 0)
    def _():
        settled[...] = jnp.zeros_like(settled)
        chunk = 128

        @pl.loop(0, bins // chunk)
        def _(part):
            at = pl.ds(pl.multiple_of(part * chunk, chunk), chunk)
            source = lax.broadcasted_iota(jnp.int32, (chunk, bins), 0) + part * chunk
            target = lax.broadcasted_iota(jnp.int32, (chunk, bins), 1)
            hit = (target <= pivots[at, :]) & (source >= 1)
            mask[at, :] = jnp.where(hit, 1.0, 0.0).astype(jnp.bfloat16)

    start = place[step]
    ahead = place[2 * radii + step]
    speed = radial[0:1, :]
    stay = 1.0 - speed
    gain = jnp.where(step == radii - 1, 0.0, speed)
    settled[half:half + cells, :] = stay * own[0] + gain * own_in[0]

    @pl.when(ahead == 0)
    def _():
        settled[0:half, :] = halo[0]
        settled[half + cells:half + cells + 1, :] = stay * edges[0, 1:2, :] + gain * edges_in[0, 1:2, :]

    @pl.when(ahead != 0)
    def _():
        settled[half - 1:half, :] = stay * edges[0, 0:1, :] + gain * edges_in[0, 0:1, :]
        settled[half + cells:, :] = halo[0]

    base = pl.multiple_of((start // 8) * 8, 8)
    turn = lax.rem(span - lax.rem(start, 8), span)
    window[...] = pltpu.roll(settled[pl.ds(base, span), :], turn, 0)
    rates[...] = pltpu.roll(jnp.broadcast_to(frag[0, pl.ds(base, span), :], (span, 128)), turn, 0)
    drift = azimuth[0:1, :]
    drifted = (
        (1.0 - jnp.abs(drift)) * window[1:1 + rows, :]
        + jnp.maximum(drift, 0.0) * window[0:rows, :]
        + jnp.maximum(-drift, 0.0) * window[2:2 + rows, :]
    )
    share = azimuth[1:2, :]
    scaled = drifted * share
    high = scaled.astype(jnp.bfloat16)
    low = (scaled - high.astype(jnp.float32)).astype(jnp.bfloat16)
    gained = jnp.dot(high, mask[...], preferred_element_type=jnp.float32)
    gained += jnp.dot(low, mask[...], preferred_element_type=jnp.float32)
    column = lax.broadcasted_iota(jnp.int32, (1, bins), 1)
    lost = jnp.where(column >= 1, 1.0, 0.0)
    broken[...] = drifted + rates[1:1 + rows, 0:1] * (gained - lost * drifted)
    far = far_ref[step]
    out[0] = (1.0 - far) * broken[1:1 + cells, :] + far * broken[0:cells, :]


def aligned_blocks(density, frag_rate, radial_speed, azimuth_speed, fraction, rest, ahead, pivots):
    radii, cells, bins = density.shape
    half = -(-(cells // 2 + 2) // 8) * 8
    before = passed(density[:, cells - 1], "phi", 1)
    after = passed(density[:, 0], "phi", -1)
    frag_before = passed(frag_rate[:, cells - half:], "phi", 1)
    frag_after = passed(frag_rate[:, :half], "phi", -1)
    edges = jnp.stack([before, after], axis=1)
    frag = jnp.concatenate([frag_before, frag_rate, frag_after], axis=1)[:, :, None]

    index = jnp.arange(radii, dtype=jnp.int32)
    same_before = (index[None, :] < index[:, None]) & (ahead[None, :] == ahead[:, None])
    forward_count = radii - jnp.sum(ahead)
    rank = jnp.sum(same_before.astype(jnp.int32), axis=1) + ahead * forward_count
    order = jnp.sum(jnp.where(rank[None, :] == index[:, None], index[None, :], 0), axis=1)
    slabs = packed(density, radial_speed, order, forward_count, half)
    halos = exchanged(slabs, forward_count)

    rows = cells + 8
    span = cells + 16
    share = 1.0 / (pivots.astype(jnp.float32) + 1.0)
    speeds = jnp.stack([azimuth_speed, share])
    place = jnp.concatenate([half - 2 - rest, rank, ahead])
    last = radii - 1
    here = lambda r, place: (r, 0, 0)
    inner = lambda r, place: (jnp.minimum(r + 1, last), 0, 0)
    fixed = lambda r, place: (0, 0)
    return pl.pallas_call(
        disc_kernel,
        grid_spec=pltpu.PrefetchScalarGridSpec(
            num_scalar_prefetch=1,
            grid=(radii,),
            in_specs=[
                pl.BlockSpec(memory_space=pltpu.SMEM),
                pl.BlockSpec((1, cells, bins), here),
                pl.BlockSpec((1, cells, bins), inner),
                pl.BlockSpec((1, half, bins), lambda r, place: (place[radii + r], 0, 0)),
                pl.BlockSpec((1, 2, bins), here),
                pl.BlockSpec((1, 2, bins), inner),
                pl.BlockSpec((1, cells + 2 * half, 1), here),
                pl.BlockSpec((1, bins), fixed),
                pl.BlockSpec((2, bins), fixed),
                pl.BlockSpec((bins, 1), fixed),
            ],
            out_specs=pl.BlockSpec((1, cells, bins), here),
            scratch_shapes=[
                pltpu.VMEM((bins, bins), jnp.bfloat16),
                pltpu.VMEM((cells + 2 * half, bins), jnp.float32),
                pltpu.VMEM((span, bins), jnp.float32),
                pltpu.VMEM((span, 128), jnp.float32),
                pltpu.VMEM((rows, bins), jnp.float32),
            ],
        ),
        out_shape=jax.ShapeDtypeStruct((radii, cells, bins), jnp.float32),
        compiler_params=pltpu.CompilerParams(vmem_limit_bytes=40 * 2**20),
        cost_estimate=pl.CostEstimate(
            flops=4 * radii * rows * bins * bins, bytes_accessed=4 * 4 * radii * cells * bins, transcendentals=0
        ),
    )(
        place, fraction, density, density, halos, edges, edges, frag,
        radial_speed[None], speeds, pivots[:, None],
    )


def carry(blocks, hops):
    radii = blocks.shape[0]
    count = lax.axis_size("phi")
    moves = [functools.partial(passed, axis="phi", by=by) for by in range(count)]

    def one(r, result):
        block = lax.dynamic_index_in_dim(result, r, 0, keepdims=False)
        landed = lax.switch(hops[r], moves, block)
        return lax.dynamic_update_index_in_dim(result, landed, r, 0)

    return lax.fori_loop(0, radii, one, blocks)


def body(density, frag_rate, radial_speed, azimuth_speed, fraction, shifts, pivots):
    cells = density.shape[1]
    count = lax.axis_size("phi")
    rest = shifts % cells
    ahead = (rest > cells // 2).astype(jnp.int32)
    hops = (shifts // cells + ahead) % count
    rest = rest - cells * ahead
    blocks = aligned_blocks(density, frag_rate, radial_speed, azimuth_speed, fraction, rest, ahead, pivots)
    return carry(blocks, hops)


def solution(mesh):
    placed = (P("disc", "phi", None), P("disc", "phi"), P(), P(), P("disc"), P("disc"), P())
    return jax.shard_map(
        body, mesh=mesh, in_specs=placed, out_specs=P("disc", "phi", None), check_vma=False
    )
```

```python
import functools
import jax
import jax.numpy as jnp
from jax import lax
from jax.experimental import pallas as pl
from jax.experimental.pallas import tpu as pltpu
from jax.sharding import PartitionSpec as P


def passed(shard, axis, by):
    count = lax.axis_size(axis)
    if by % count == 0:
        return shard
    return lax.ppermute(shard, axis, [(i, (i + by) % count) for i in range(count)])


def pack_kernel(half, ends, place, own, own_in, frag, radial, out):
    slot = pl.program_id(0)
    radii = pl.num_programs(0)
    cells = own.shape[1]
    r = place[slot]
    forward = slot < place[radii]
    first = pl.multiple_of(jnp.where(forward, cells - half, 0), 8)
    speed = radial[0:1, :]
    stay = 1.0 - speed
    gain = jnp.where(r == radii - 1, 0.0, speed)
    rows = pl.ds(first, half)
    at = pl.multiple_of(ends + slot * half, 8)
    out[pl.ds(at, half), :] = stay * own[0, rows, :] + gain * own_in[0, rows, :]

    @pl.when(forward)
    def _():
        out[pl.ds(at, 1), :] = frag[0, 0:1, :]

    @pl.when(jnp.logical_not(forward))
    def _():
        out[pl.ds(at + half - 1, 1), :] = frag[0, 1:2, :]

    final = out.shape[0] - ends
    out[pl.ds(r, 1), :] = stay * own[0, cells - 1:cells, :] + gain * own_in[0, cells - 1:cells, :]
    out[pl.ds(final + r, 1), :] = stay * own[0, 0:1, :] + gain * own_in[0, 0:1, :]


def packed(density, frag_rate, radial_speed, order, forward_count, half, ends):
    radii, cells, bins = density.shape
    last = radii - 1
    total = 2 * ends + radii * half
    place = jnp.concatenate([order, forward_count[None]])
    wide = ((0, 0), (0, bins - half))
    frag = jnp.stack([jnp.pad(frag_rate[:, cells - half:], wide), jnp.pad(frag_rate[:, :half], wide)], axis=1)
    return pl.pallas_call(
        functools.partial(pack_kernel, half, ends),
        grid_spec=pltpu.PrefetchScalarGridSpec(
            num_scalar_prefetch=1,
            grid=(radii,),
            in_specs=[
                pl.BlockSpec((1, cells, bins), lambda j, place: (place[j], 0, 0)),
                pl.BlockSpec((1, cells, bins), lambda j, place: (jnp.minimum(place[j] + 1, last), 0, 0)),
                pl.BlockSpec((1, 2, bins), lambda j, place: (place[j], 0, 0)),
                pl.BlockSpec((1, bins), lambda j, place: (0, 0)),
            ],
            out_specs=pl.BlockSpec((total, bins), lambda j, place: (0, 0)),
        ),
        out_shape=jax.ShapeDtypeStruct((total, bins), jnp.float32),
        compiler_params=pltpu.CompilerParams(vmem_limit_bytes=32 * 2**20),
        cost_estimate=pl.CostEstimate(
            flops=3 * radii * half * bins, bytes_accessed=10 * radii * cells * bins, transcendentals=0
        ),
    )(place, density, density, frag, radial_speed[None])


def exchanged(slabs, forward_count, radii, half, ends):
    def move(forward, slabs):
        cut = ends + forward * half
        return jnp.concatenate([passed(slabs[:cut], "phi", 1), passed(slabs[cut:], "phi", -1)], axis=0)

    return lax.switch(forward_count, [functools.partial(move, n) for n in range(radii + 1)], slabs)


def disc_kernel(
    half, ends, place, far_ref, own, own_in, arrived, frag, radial, azimuth, pivots,
    out, mask, settled, rates, window, turned, broken,
):
    step = pl.program_id(0)
    radii = pl.num_programs(0)
    cells, bins = own.shape[1:]
    rows = broken.shape[0]
    span = window.shape[0]

    @pl.when(step == 0)
    def _():
        settled[...] = jnp.zeros_like(settled)
        rates[...] = jnp.zeros_like(rates)
        chunk = 128

        @pl.loop(0, bins // chunk)
        def _(part):
            at = pl.ds(pl.multiple_of(part * chunk, chunk), chunk)
            source = lax.broadcasted_iota(jnp.int32, (chunk, bins), 0) + part * chunk
            target = lax.broadcasted_iota(jnp.int32, (chunk, bins), 1)
            hit = (target <= pivots[at, :]) & (source >= 1)
            mask[at, :] = jnp.where(hit, 1.0, 0.0).astype(jnp.bfloat16)

    start = place[step]
    slab = pl.multiple_of(ends + place[radii + step] * half, 8)
    ahead = place[2 * radii + step]
    speed = radial[0:1, :]
    gain = jnp.where(step == radii - 1, 0.0, speed)
    settled[half:half + cells, :] = (1.0 - speed) * own[0] + gain * own_in[0]
    rates[half:half + cells, :] = jnp.broadcast_to(frag[0], (cells, 128))

    def column(at, row):
        group = arrived[pl.ds(pl.multiple_of(at, 8), 8), :]
        return jnp.transpose(jnp.broadcast_to(group[row:row + 1, 0:128], (128, 128)))[0:half, :]

    @pl.when(ahead == 0)
    def _():
        settled[0:half, :] = arrived[pl.ds(slab, half), :]
        settled[half + cells:half + cells + 1, :] = arrived[pl.ds(arrived.shape[0] - ends + step, 1), :]
        rates[0:half, :] = column(slab, 0)

    @pl.when(ahead != 0)
    def _():
        settled[half - 1:half, :] = arrived[pl.ds(step, 1), :]
        settled[half + cells:, :] = arrived[pl.ds(slab, half), :]
        rates[half + cells:, :] = column(slab + half - 8, 7)

    base = pl.multiple_of((start // 8) * 8, 8)
    turn = lax.rem(span - lax.rem(start, 8), span)
    window[...] = pltpu.roll(settled[pl.ds(base, span), :], turn, 0)
    turned[...] = pltpu.roll(rates[pl.ds(base, span), :], turn, 0)
    drift = azimuth[0:1, :]
    drifted = (
        (1.0 - jnp.abs(drift)) * window[1:1 + rows, :]
        + jnp.maximum(drift, 0.0) * window[0:rows, :]
        + jnp.maximum(-drift, 0.0) * window[2:2 + rows, :]
    )
    share = azimuth[1:2, :]
    scaled = drifted * share
    high = scaled.astype(jnp.bfloat16)
    low = (scaled - high.astype(jnp.float32)).astype(jnp.bfloat16)
    gained = jnp.dot(high, mask[...], preferred_element_type=jnp.float32)
    gained += jnp.dot(low, mask[...], preferred_element_type=jnp.float32)
    lane = lax.broadcasted_iota(jnp.int32, (1, bins), 1)
    lost = jnp.where(lane >= 1, 1.0, 0.0)
    broken[...] = drifted + turned[1:1 + rows, 0:1] * (gained - lost * drifted)
    far = far_ref[step]
    out[0] = (1.0 - far) * broken[1:1 + cells, :] + far * broken[0:cells, :]


def aligned_blocks(density, frag_rate, radial_speed, azimuth_speed, fraction, rest, ahead, pivots):
    radii, cells, bins = density.shape
    half = -(-(cells // 2 + 2) // 8) * 8
    ends = -(-radii // 8) * 8

    index = jnp.arange(radii, dtype=jnp.int32)
    same_before = (index[None, :] < index[:, None]) & (ahead[None, :] == ahead[:, None])
    forward_count = radii - jnp.sum(ahead)
    rank = jnp.sum(same_before.astype(jnp.int32), axis=1) + ahead * forward_count
    order = jnp.sum(jnp.where(rank[None, :] == index[:, None], index[None, :], 0), axis=1)
    slabs = packed(density, frag_rate, radial_speed, order, forward_count, half, ends)
    arrived = exchanged(slabs, forward_count, radii, half, ends)

    rows = cells + 8
    span = cells + 16
    share = 1.0 / (pivots.astype(jnp.float32) + 1.0)
    speeds = jnp.stack([azimuth_speed, share])
    place = jnp.concatenate([half - 2 - rest, rank, ahead])
    last = radii - 1
    here = lambda r, place: (r, 0, 0)
    inner = lambda r, place: (jnp.minimum(r + 1, last), 0, 0)
    fixed = lambda r, place: (0, 0)
    return pl.pallas_call(
        functools.partial(disc_kernel, half, ends),
        grid_spec=pltpu.PrefetchScalarGridSpec(
            num_scalar_prefetch=1,
            grid=(radii,),
            in_specs=[
                pl.BlockSpec(memory_space=pltpu.SMEM),
                pl.BlockSpec((1, cells, bins), here),
                pl.BlockSpec((1, cells, bins), inner),
                pl.BlockSpec(arrived.shape, fixed),
                pl.BlockSpec((1, cells, 1), here),
                pl.BlockSpec((1, bins), fixed),
                pl.BlockSpec((2, bins), fixed),
                pl.BlockSpec((bins, 1), fixed),
            ],
            out_specs=pl.BlockSpec((1, cells, bins), here),
            scratch_shapes=[
                pltpu.VMEM((bins, bins), jnp.bfloat16),
                pltpu.VMEM((cells + 2 * half, bins), jnp.float32),
                pltpu.VMEM((cells + 2 * half, 128), jnp.float32),
                pltpu.VMEM((span, bins), jnp.float32),
                pltpu.VMEM((span, 128), jnp.float32),
                pltpu.VMEM((rows, bins), jnp.float32),
            ],
        ),
        out_shape=jax.ShapeDtypeStruct((radii, cells, bins), jnp.float32),
        compiler_params=pltpu.CompilerParams(vmem_limit_bytes=40 * 2**20),
        cost_estimate=pl.CostEstimate(
            flops=4 * radii * rows * bins * bins, bytes_accessed=4 * 4 * radii * cells * bins, transcendentals=0
        ),
    )(
        place, fraction, density, density, arrived, frag_rate[:, :, None],
        radial_speed[None], speeds, pivots[:, None],
    )


def carry(blocks, hops):
    radii = blocks.shape[0]
    count = lax.axis_size("phi")
    moves = [functools.partial(passed, axis="phi", by=by) for by in range(count)]

    def one(r, result):
        block = lax.dynamic_index_in_dim(result, r, 0, keepdims=False)
        landed = lax.switch(hops[r], moves, block)
        return lax.dynamic_update_index_in_dim(result, landed, r, 0)

    return lax.fori_loop(0, radii, one, blocks)


def body(density, frag_rate, radial_speed, azimuth_speed, fraction, shifts, pivots):
    cells = density.shape[1]
    count = lax.axis_size("phi")
    rest = shifts % cells
    ahead = (rest > cells // 2).astype(jnp.int32)
    hops = (shifts // cells + ahead) % count
    rest = rest - cells * ahead
    blocks = aligned_blocks(density, frag_rate, radial_speed, azimuth_speed, fraction, rest, ahead, pivots)
    return carry(blocks, hops)


def solution(mesh):
    placed = (P("disc", "phi", None), P("disc", "phi"), P(), P(), P("disc"), P("disc"), P())
    return jax.shard_map(
        body, mesh=mesh, in_specs=placed, out_specs=P("disc", "phi", None), check_vma=False
    )
```
